32 devices in a mesh: section: 4 (over z), seq: 8 (over y, x, core).
Axes of the slice: x: 2, y: 2, z: 4, core: 2. Of those that a mesh axis runs over, the one named last changes fastest.
Arguments:
- bases: int32 [4, 262144], P(None, 'seq'), may hold values from 0 to 3
- stem_weight: bfloat16 [512, 1536], replicated, may hold values from -0.5 to 0.5
- norm_gain: float32 [4, 1536], P('section'), may hold values from 0.25 to 1.75
- conv_taps: float32 [4, 5, 1536], P('section'), may hold values from -2.7 to 2.7
- proj_weight: bfloat16 [4, 1536, 1536], P('section'), may hold values from -0.15625 to 0.15625
- dest: int32 [256], P('seq'), may hold values from 0 to 255, as said below
Outputs:
- hints: bfloat16 [4, 4, 2048, 1536], P('section', None, 'seq')
The draws below stay inside these ranges and needn't reach their ends.
Inputs may be any that keep to these rules, and one draw needn't show every extreme that they name: dest is a permutation. Slot dest[r] belongs to owner dest[r] // 32; the runs of one index d of seq (r from d * 32) go to every owner in equal numbers, 4 each, and (dest[r] % 32) // 4 equals d.
All inputs are finite; a program needn't handle non-finite values.
Results may differ from the reference program's by a relative error of at most 0.007.
Values may be sent and summed in bfloat16 or wider, within the bound.
A program may use at most 64 MiB of HBM per device.

```python
import jax
import jax.numpy as jnp
from jax import lax

C = 1536
TAPS = 5
BLOCK_BP = 128
SEG = 8
MICRO = 4
SECTIONS = 4
BLOCKS = 2048
BP = 262144
SEGS_DEV = 32
SEGS = 256
SHARE = 4


def draw_dest(key, part):
    sources = SEGS // SEGS_DEV
    key_list = jax.random.split(key, sources)
    orders = jax.vmap(lambda one_key: jax.random.permutation(one_key, SEGS_DEV))(key_list)
    orders = orders.astype(jnp.int32)
    source_idx = jnp.arange(sources, dtype=jnp.int32)[:, None]
    owners = orders % sources
    within = orders // sources
    slots = owners * SEGS_DEV + source_idx * SHARE + within
    return slots.reshape(-1).astype(jnp.int32)


def place_ends(array, key, least, high):
    index_at = [jax.random.randint(jax.random.fold_in(key, axis), (), 0, length) for axis, length in enumerate(array.shape)]
    main_axis = array.shape.index(max(array.shape))
    next_to = index_at[:main_axis] + [(index_at[main_axis] + 1) % array.shape[main_axis]] + index_at[main_axis + 1:]
    return array.at[tuple(index_at)].set(least).at[tuple(next_to)].set(high)


def level_of(own_key, shape, cuts, smallest, high):
    level = 1.0
    for axis_at, shards_of in cuts:
        draws = jax.random.uniform(jax.random.fold_in(jax.random.fold_in(own_key, 6), axis_at), (shards_of,), jnp.float32, smallest / len(cuts), high / len(cuts))
        level = level * jnp.repeat(jnp.exp(draws), shape[axis_at] // shards_of).reshape((-1,) + (1,) * (len(shape) - 1 - axis_at))
    return level


def centred(rng, shape, deviation, bound, shards=(), kind=jnp.bfloat16):
    result = deviation * jax.random.normal(rng, shape, jnp.float32)
    if shards:
        result = result * level_of(rng, shape, shards, -0.22, 0.18)
    return jnp.clip(result, -bound, bound).astype(kind)


def setup_inputs(seed: int = 0) -> dict:
    keys = jax.random.split(jax.random.key(seed), 7)
    bases = place_ends(jax.random.randint(keys[0], (MICRO, BP), 0, 4), jax.random.fold_in(keys[0], 1), 0, 3).astype(jnp.int32)
    stem_weight = centred(keys[1], (BLOCK_BP * 4, C), BLOCK_BP ** -0.5, 0.5)
    norm_gain = jnp.clip(1.0 + 0.15 * jax.random.normal(keys[2], (SECTIONS, C), jnp.float32), 0.25, 1.75)
    conv_taps = centred(keys[3], (SECTIONS, TAPS, C), 0.45, 2.7, ((0, 4),), jnp.float32)
    proj_weight = centred(keys[4], (SECTIONS, C, C), C ** -0.5, 0.15625, ((0, 4),))
    dest = draw_dest(jax.random.fold_in(keys[6], 71), 0)
    return {"bases": bases, "stem_weight": stem_weight, "norm_gain": norm_gain, "conv_taps": conv_taps, "proj_weight": proj_weight, "dest": dest}


def section_block(current, gain_row, tap_rows, weight):
    wide_state = current.astype(jnp.float32)
    inv_rms = lax.rsqrt(lax.optimization_barrier(jnp.mean(wide_state * wide_state, axis=-1, keepdims=True)) + 1e-06)
    normed = (wide_state * inv_rms * gain_row).astype(jnp.bfloat16)
    reach = tap_rows.shape[0] // 2
    padded = jnp.pad(normed, ((reach, reach), (0, 0)))
    length = current.shape[0]
    mixed = jnp.zeros(current.shape, jnp.float32)
    for offset in range(tap_rows.shape[0]):
        mixed = mixed + tap_rows[offset] * padded[offset:offset + length].astype(jnp.float32)
    mixed = mixed.astype(jnp.bfloat16)
    update = jnp.dot(mixed, weight, preferred_element_type=jnp.float32)
    return (wide_state + jax.nn.gelu(update)).astype(jnp.bfloat16)

def reference(bases, stem_weight, norm_gain, conv_taps, proj_weight, dest):

    def one_window(base_codes):
        blocks = base_codes.reshape(BLOCKS, BLOCK_BP)
        onehot = (blocks[:, :, None] == jnp.arange(4, dtype=jnp.int32)).astype(jnp.bfloat16)
        onehot = onehot.reshape(BLOCKS, BLOCK_BP * 4)
        current = jnp.dot(onehot, stem_weight, preferred_element_type=jnp.float32).astype(jnp.bfloat16)
        section_hints = []
        for section_num in range(SECTIONS):
            current = section_block(current, norm_gain[section_num], conv_taps[section_num], proj_weight[section_num])
            section_hints.append(current)
        pieces = jnp.stack(section_hints).reshape(SECTIONS, SEGS, SEG, C)
        placed = jnp.zeros_like(pieces).at[:, dest].set(pieces)
        return placed.reshape(SECTIONS, BLOCKS, C)
    all_hints = lax.map(one_window, bases)
    return jnp.transpose(all_hints, (1, 0, 2, 3))
```

```python
import functools

import jax
import jax.numpy as jnp
from jax import lax
from jax.experimental import pallas as pl
from jax.experimental.pallas import tpu as pltpu
from jax.sharding import PartitionSpec as P

BLOCK_BP = 128
CHUNK = 64
LEAD = 8
MESH = pl.DeviceIdType.MESH


def kernel(
    sizes,
    bases_ref,
    stem_ref,
    gain_ref,
    taps_ref,
    weight_ref,
    order_ref,
    out_ref,
    codes,
    arriving,
    leaving,
    ordered,
    state_buf,
    normed_buf,
    mixed_buf,
    codes_send,
    codes_recv,
    local_sem,
    state_send,
    state_recv,
    hint_send,
    hint_recv,
    own_sem,
):
    micro, rows, halo, sections, peers, reach = sizes
    channels = weight_ref.shape[1]
    span = rows + 2 * halo
    chunks = micro * span // CHUNK
    share = rows // peers
    taps = 2 * reach + 1
    sec = lax.axis_index("section")
    me = lax.axis_index("seq")
    first, last = sec == 0, sec == sections - 1
    col_tile = 256
    out_tile = 512

    barrier = pltpu.get_barrier_semaphore()

    def greet(k, carry):
        pl.semaphore_signal(
            barrier, inc=1, device_id={"seq": lax.rem(me + k, peers)}, device_id_type=MESH
        )
        return carry

    lax.fori_loop(1, peers, greet, 0)

    @pl.when(sec > 0)
    def _():
        pl.semaphore_signal(barrier, inc=1, device_id={"section": sec - 1}, device_id_type=MESH)

    @pl.when(last)
    def _():
        pl.semaphore_wait(barrier, peers - 1)

    @pl.when(jnp.logical_not(last))
    def _():
        pl.semaphore_wait(barrier, peers)

    state_buf[0:LEAD] = jnp.zeros((LEAD, channels), jnp.float32)
    normed_buf[0:LEAD] = jnp.zeros((LEAD, channels), jnp.float32)

    def to_right(m):
        return pltpu.make_async_remote_copy(
            src_ref=bases_ref.at[m, pl.ds(rows - halo, halo)],
            dst_ref=codes.at[pl.ds(m * span, halo)],
            send_sem=codes_send.at[0, m],
            recv_sem=codes_recv.at[0, m],
            device_id={"seq": me + 1},
            device_id_type=MESH,
        )

    def to_left(m):
        return pltpu.make_async_remote_copy(
            src_ref=bases_ref.at[m, pl.ds(0, halo)],
            dst_ref=codes.at[pl.ds(m * span + halo + rows, halo)],
            send_sem=codes_send.at[1, m],
            recv_sem=codes_recv.at[1, m],
            device_id={"seq": me - 1},
            device_id_type=MESH,
        )

    @pl.when(first)
    def _():
        @pl.when(me < peers - 1)
        def _():
            for m in range(micro):
                to_right(m).start()

        @pl.when(me > 0)
        def _():
            for m in range(micro):
                to_left(m).start()

        for m in range(micro):
            codes[m * span + halo : m * span + halo + rows] = bases_ref[m]

        @pl.when(me == 0)
        def _():
            for m in range(micro):
                codes[m * span : m * span + halo] = jnp.zeros((halo, BLOCK_BP), jnp.int32)

        @pl.when(me == peers - 1)
        def _():
            for m in range(micro):
                low = m * span + halo + rows
                codes[low : low + halo] = jnp.zeros((halo, BLOCK_BP), jnp.int32)

        @pl.when(me < peers - 1)
        def _():
            for m in range(micro):
                to_right(m).wait_send()
                to_left(m).wait_recv()

        @pl.when(me > 0)
        def _():
            for m in range(micro):
                to_left(m).wait_send()
                to_right(m).wait_recv()

    def state_copy(i):
        part = pl.ds(pl.multiple_of(i * CHUNK, CHUNK), CHUNK)
        return pltpu.make_async_remote_copy(
            src_ref=leaving.at[part],
            dst_ref=arriving.at[part],
            send_sem=state_send.at[i],
            recv_sem=state_recv.at[i],
            device_id={"section": sec + 1},
            device_id_type=MESH,
        )

    def hint_copy(m, k):
        peer = lax.rem(me + k, peers)
        return pltpu.make_async_remote_copy(
            src_ref=ordered.at[m, peer],
            dst_ref=out_ref.at[m, me],
            send_sem=hint_send.at[m, k - 1],
            recv_sem=hint_recv.at[m, k - 1],
            device_id={"seq": peer},
            device_id_type=MESH,
        )

    def own_copy(m):
        return pltpu.make_async_copy(ordered.at[m, me], out_ref.at[m, me], own_sem.at[m])

    def step(i, carry):
        base = pl.multiple_of(i * CHUNK, CHUNK)
        state_buf[0:LEAD] = state_buf[CHUNK : CHUNK + LEAD]
        normed_buf[0:LEAD] = normed_buf[CHUNK : CHUNK + LEAD]

        @pl.when(first)
        def _():
            code = codes[pl.ds(base, CHUNK)].astype(jnp.bfloat16)
            wide = 4 * BLOCK_BP
            spread = (
                lax.broadcasted_iota(jnp.int32, (BLOCK_BP, wide), 1) // 4
                == lax.broadcasted_iota(jnp.int32, (BLOCK_BP, wide), 0)
            )
            spread = jnp.where(spread, 1.0, 0.0).astype(jnp.bfloat16)
            repeated = jnp.dot(code, spread, preferred_element_type=jnp.float32)
            letter = lax.broadcasted_iota(jnp.int32, (CHUNK, wide), 1) % 4
            onehot = jnp.where(repeated == letter.astype(jnp.float32), 1.0, 0.0)
            onehot = onehot.astype(jnp.bfloat16)
            for c in range(0, channels, out_tile):
                part = jnp.dot(
                    onehot, stem_ref[:, c : c + out_tile], preferred_element_type=jnp.float32
                )
                state_buf[LEAD : LEAD + CHUNK, c : c + out_tile] = part.astype(
                    jnp.bfloat16
                ).astype(jnp.float32)

        @pl.when(jnp.logical_not(first))
        def _():
            state_copy(i).wait_recv()
            for c in range(0, channels, col_tile):
                state_buf[LEAD : LEAD + CHUNK, c : c + col_tile] = arriving[
                    pl.ds(base, CHUNK), c : c + col_tile
                ].astype(jnp.float32)

        total = jnp.zeros((CHUNK, 128), jnp.float32)
        for c in range(0, channels, 128):
            part = state_buf[LEAD : LEAD + CHUNK, c : c + 128]
            total = total + part * part
        mean = jnp.sum(total, axis=-1, keepdims=True) * (1.0 / channels)
        inv_rms = lax.rsqrt(mean + 1e-06)
        place = lax.broadcasted_iota(jnp.int32, (CHUNK, 1), 0) + (base - reach * sec)
        low_end = (place >= 0) & (place < halo)
        high_end = (place >= span - halo) & (place < span)
        for m in range(1, micro):
            at = m * span
            low_end = low_end | ((place >= at) & (place < at + halo))
            high_end = high_end | ((place >= at + span - halo) & (place < at + span))
        outside = (low_end & (me == 0)) | (high_end & (me == peers - 1))
        inv_rms = jnp.where(outside, 0.0, inv_rms)

        for c in range(0, channels, col_tile):
            cols = slice(c, c + col_tile)
            normed = state_buf[LEAD : LEAD + CHUNK, cols] * inv_rms * gain_ref[:, cols]
            normed_buf[LEAD : LEAD + CHUNK, cols] = normed.astype(jnp.bfloat16).astype(jnp.float32)
            mixed = jnp.zeros((CHUNK, col_tile), jnp.float32)
            for k in range(taps):
                low = LEAD - 2 * reach + k
                mixed = mixed + taps_ref[0, k : k + 1, cols] * normed_buf[low : low + CHUNK, cols]
            mixed_buf[:, cols] = mixed.astype(jnp.bfloat16)

        for c in range(0, channels, out_tile):
            cols = slice(c, c + out_tile)
            update = jnp.dot(
                mixed_buf[...], weight_ref[0, :, cols], preferred_element_type=jnp.float32
            )
            low = LEAD - reach
            result = state_buf[low : low + CHUNK, cols] + jax.nn.gelu(update)
            leaving[pl.ds(base, CHUNK), cols] = result.astype(jnp.bfloat16)

        @pl.when(jnp.logical_not(last))
        def _():
            state_copy(i).start()

        m = (i * CHUNK) // span

        @pl.when(((i + 1) * CHUNK) // span > m)
        def _():
            top = pl.multiple_of(m * span, 16)
            for c in range(0, channels, out_tile):
                cols = slice(c, c + out_tile)
                moved = jnp.dot(
                    order_ref[...],
                    leaving[pl.ds(top, span), cols],
                    preferred_element_type=jnp.float32,
                )
                ordered[m, :, :, cols] = moved.astype(jnp.bfloat16).reshape(
                    peers, share, out_tile
                )

            def send(k, carry):
                hint_copy(m, k).start()
                return carry

            lax.fori_loop(1, peers, send, 0)
            own_copy(m).start()

        return carry

    lax.fori_loop(0, chunks, step, 0)

    @pl.when(jnp.logical_not(last))
    def _():
        def drain(i, carry):
            state_copy(i).wait_send()
            return carry

        lax.fori_loop(0, chunks, drain, 0)

    for m in range(micro):
        def finish(k, carry):
            copy = hint_copy(m, k)
            copy.wait_send()
            copy.wait_recv()
            return carry

        lax.fori_loop(1, peers, finish, 0)
        own_copy(m).wait()


def on_device(bases, stem_weight, norm_gain, conv_taps, proj_weight, dest):
    micro = bases.shape[0]
    rows = bases.shape[1] // BLOCK_BP
    channels = stem_weight.shape[1]
    sections = lax.axis_size("section")
    peers = lax.axis_size("seq")
    segs_dev = dest.shape[0]
    per_peer = segs_dev // peers
    seg_rows = rows // segs_dev
    share = rows // peers
    reach = conv_taps.shape[1] // 2
    halo = reach * sections
    span = rows + 2 * halo
    chunks = micro * span // CHUNK
    assert halo % 8 == 0 and (micro * span) % CHUNK == 0 and CHUNK <= span
    assert 2 * reach <= LEAD

    send_slot = dest // segs_dev * per_peer + dest % segs_dev % per_peer
    place = jnp.arange(seg_rows, dtype=jnp.int32)
    target = (send_slot[:, None] * seg_rows + place[None, :]).reshape(rows)
    lag = halo + reach * (lax.axis_index("section") + 1)
    from_row = jnp.arange(rows, dtype=jnp.int32) + lag
    by_target = target[:, None] == jnp.arange(rows, dtype=jnp.int32)[None, :]
    by_source = from_row[:, None] == jnp.arange(span, dtype=jnp.int32)[None, :]
    order = jnp.dot(
        by_target.astype(jnp.bfloat16).T,
        by_source.astype(jnp.bfloat16),
        preferred_element_type=jnp.float32,
    ).astype(jnp.bfloat16)

    vmem = pl.BlockSpec(memory_space=pltpu.VMEM)
    dma = pltpu.SemaphoreType.DMA
    hints = pl.pallas_call(
        functools.partial(kernel, (micro, rows, halo, sections, peers, reach)),
        out_shape=jax.ShapeDtypeStruct((micro, peers, share, channels), jnp.bfloat16),
        in_specs=[vmem] * 6,
        out_specs=vmem,
        scratch_shapes=[
            pltpu.VMEM((micro * span, BLOCK_BP), jnp.int32),
            pltpu.VMEM((micro * span, channels), jnp.bfloat16),
            pltpu.VMEM((micro * span, channels), jnp.bfloat16),
            pltpu.VMEM((micro, peers, share, channels), jnp.bfloat16),
            pltpu.VMEM((LEAD + CHUNK, channels), jnp.float32),
            pltpu.VMEM((LEAD + CHUNK, channels), jnp.float32),
            pltpu.VMEM((CHUNK, channels), jnp.bfloat16),
            dma((2, micro)),
            dma((2, micro)),
            dma,
            dma((chunks,)),
            dma((chunks,)),
            dma((micro, peers - 1)),
            dma((micro, peers - 1)),
            dma((micro,)),
        ],
        compiler_params=pltpu.CompilerParams(
            collective_id=0, has_side_effects=True, vmem_limit_bytes=48 * 1024 * 1024
        ),
    )(
        bases.reshape(micro, rows, BLOCK_BP),
        stem_weight,
        norm_gain,
        conv_taps,
        proj_weight,
        order,
    )
    return hints.reshape(1, micro, rows, channels)


def solution(mesh):
    return jax.shard_map(
        on_device,
        mesh=mesh,
        in_specs=(
            P(None, "seq"),
            P(),
            P("section", None),
            P("section", None, None),
            P("section", None, None),
            P("seq"),
        ),
        out_specs=P("section", None, "seq", None),
        check_vma=False,
    )
```

```python
import functools

import jax
import jax.numpy as jnp
from jax import lax
from jax.experimental import pallas as pl
from jax.experimental.pallas import tpu as pltpu
from jax.sharding import PartitionSpec as P

BLOCK_BP = 128
CHUNK = 32
LEAD = 8
MESH = pl.DeviceIdType.MESH


def kernel(
    sizes,
    bases_ref,
    stem_hbm,
    gain_hbm,
    taps_hbm,
    weight_hbm,
    dest_ref,
    out_ref,
    stem_ref,
    gain_ref,
    taps_ref,
    weight_ref,
    order_ref,
    codes,
    arriving,
    leaving,
    ordered,
    state_buf,
    normed_buf,
    mixed_buf,
    codes_send,
    codes_recv,
    local_sem,
    state_send,
    state_recv,
    hint_send,
    hint_recv,
    own_sem,
):
    micro, rows, halo, sections, peers, reach = sizes
    channels = weight_ref.shape[1]
    segs_dev = dest_ref.shape[1]
    per_peer = segs_dev // peers
    seg_rows = rows // segs_dev
    span = rows + 2 * halo
    chunks = micro * span // CHUNK
    share = rows // peers
    taps = 2 * reach + 1
    sec = lax.axis_index("section")
    me = lax.axis_index("seq")
    first, last = sec == 0, sec == sections - 1
    col_tile = 256
    out_tile = 512

    loads = [
        pltpu.make_async_copy(src, dst, local_sem.at[n])
        for n, (src, dst) in enumerate(
            (
                (gain_hbm, gain_ref),
                (taps_hbm, taps_ref),
                (stem_hbm, stem_ref),
                (weight_hbm, weight_ref),
            )
        )
    ]
    for load in loads:
        load.start()

    barrier = pltpu.get_barrier_semaphore()

    def greet(k, carry):
        pl.semaphore_signal(
            barrier, inc=1, device_id={"seq": lax.rem(me + k, peers)}, device_id_type=MESH
        )
        return carry

    lax.fori_loop(1, peers, greet, 0)

    @pl.when(sec > 0)
    def _():
        pl.semaphore_signal(barrier, inc=1, device_id={"section": sec - 1}, device_id_type=MESH)

    @pl.when(first)
    def _():
        for m in range(micro):
            codes[m * span + halo : m * span + halo + rows] = bases_ref[:, m, :]

    state_buf[CHUNK : CHUNK + LEAD] = jnp.zeros((LEAD, channels), jnp.float32)
    normed_buf[CHUNK : CHUNK + LEAD] = jnp.zeros((LEAD, channels), jnp.float32)

    @pl.when(last)
    def _():
        pl.semaphore_wait(barrier, peers - 1)

    @pl.when(jnp.logical_not(last))
    def _():
        pl.semaphore_wait(barrier, peers)

    def to_right(m):
        return pltpu.make_async_remote_copy(
            src_ref=codes.at[pl.ds(m * span + rows, halo)],
            dst_ref=codes.at[pl.ds(m * span, halo)],
            send_sem=codes_send.at[0, m],
            recv_sem=codes_recv.at[0, m],
            device_id={"seq": me + 1},
            device_id_type=MESH,
        )

    def to_left(m):
        return pltpu.make_async_remote_copy(
            src_ref=codes.at[pl.ds(m * span + halo, halo)],
            dst_ref=codes.at[pl.ds(m * span + halo + rows, halo)],
            send_sem=codes_send.at[1, m],
            recv_sem=codes_recv.at[1, m],
            device_id={"seq": me - 1},
            device_id_type=MESH,
        )

    @pl.when(first)
    def _():
        @pl.when(me < peers - 1)
        def _():
            for m in range(micro):
                to_right(m).start()

        @pl.when(me > 0)
        def _():
            for m in range(micro):
                to_left(m).start()

        @pl.when(me == 0)
        def _():
            for m in range(micro):
                codes[m * span : m * span + halo] = jnp.zeros((halo, BLOCK_BP), jnp.int32)

        @pl.when(me == peers - 1)
        def _():
            for m in range(micro):
                low = m * span + halo + rows
                codes[low : low + halo] = jnp.zeros((halo, BLOCK_BP), jnp.int32)

        @pl.when(me < peers - 1)
        def _():
            for m in range(micro):
                to_right(m).wait_send()
                to_left(m).wait_recv()

        @pl.when(me > 0)
        def _():
            for m in range(micro):
                to_left(m).wait_send()
                to_right(m).wait_recv()

    iota = functools.partial(lax.broadcasted_iota, jnp.int32)

    def zero_one(flags):
        return jnp.where(flags, 1.0, 0.0).astype(jnp.bfloat16)

    def build_order():
        dest_row = dest_ref[...]
        slot = lax.div(dest_row, segs_dev) * per_peer + lax.rem(
            lax.rem(dest_row, segs_dev), per_peer
        )
        runs = zero_one(iota((segs_dev, segs_dev), 0) == slot)
        by_slot = zero_one(
            lax.div(iota((rows, segs_dev), 0), seg_rows) == iota((rows, segs_dev), 1)
        )
        lag = halo + reach * (sec + 1)
        source = iota((segs_dev, span), 1) - lag
        by_run = zero_one(
            (source >= 0)
            & (lax.div(jnp.maximum(source, 0), seg_rows) == iota((segs_dev, span), 0))
        )
        picked = jnp.dot(by_slot, runs, preferred_element_type=jnp.float32).astype(jnp.bfloat16)
        picked = jnp.dot(picked, by_run, preferred_element_type=jnp.float32)
        phase = lax.rem(
            iota((rows, span), 0) - iota((rows, span), 1) + (lag + seg_rows * span), seg_rows
        )
        order_ref[...] = jnp.where(phase == 0, picked, 0.0).astype(jnp.bfloat16)

    def state_copy(i):
        part = pl.ds(pl.multiple_of(i * CHUNK, CHUNK), CHUNK)
        return pltpu.make_async_remote_copy(
            src_ref=leaving.at[part],
            dst_ref=arriving.at[part],
            send_sem=state_send.at[i],
            recv_sem=state_recv.at[i],
            device_id={"section": sec + 1},
            device_id_type=MESH,
        )

    def hint_copy(m, k):
        peer = lax.rem(me + k, peers)
        return pltpu.make_async_remote_copy(
            src_ref=ordered.at[m, peer],
            dst_ref=out_ref.at[m, me],
            send_sem=hint_send.at[m, k - 1],
            recv_sem=hint_recv.at[m, k - 1],
            device_id={"seq": peer},
            device_id_type=MESH,
        )

    def own_copy(m):
        return pltpu.make_async_copy(ordered.at[m, me], out_ref.at[m, me], own_sem.at[m])

    def step(i, carry):
        base = pl.multiple_of(i * CHUNK, CHUNK)
        state_buf[0:LEAD] = state_buf[CHUNK : CHUNK + LEAD]
        normed_buf[0:LEAD] = normed_buf[CHUNK : CHUNK + LEAD]

        @pl.when(first)
        def _():
            code = codes[pl.ds(base, CHUNK)].astype(jnp.bfloat16)
            wide = 4 * BLOCK_BP
            spread = (
                lax.broadcasted_iota(jnp.int32, (BLOCK_BP, wide), 1) // 4
                == lax.broadcasted_iota(jnp.int32, (BLOCK_BP, wide), 0)
            )
            spread = jnp.where(spread, 1.0, 0.0).astype(jnp.bfloat16)
            repeated = jnp.dot(code, spread, preferred_element_type=jnp.float32)
            letter = lax.broadcasted_iota(jnp.int32, (CHUNK, wide), 1) % 4
            onehot = jnp.where(repeated == letter.astype(jnp.float32), 1.0, 0.0)
            onehot = onehot.astype(jnp.bfloat16)
            for c in range(0, channels, out_tile):
                part = jnp.dot(
                    onehot, stem_ref[:, c : c + out_tile], preferred_element_type=jnp.float32
                )
                state_buf[LEAD : LEAD + CHUNK, c : c + out_tile] = part.astype(
                    jnp.bfloat16
                ).astype(jnp.float32)

        @pl.when(jnp.logical_not(first))
        def _():
            state_copy(i).wait_recv()
            for c in range(0, channels, col_tile):
                state_buf[LEAD : LEAD + CHUNK, c : c + col_tile] = arriving[
                    pl.ds(base, CHUNK), c : c + col_tile
                ].astype(jnp.float32)

        total = jnp.zeros((CHUNK, 128), jnp.float32)
        for c in range(0, channels, 128):
            part = state_buf[LEAD : LEAD + CHUNK, c : c + 128]
            total = total + part * part
        mean = jnp.sum(total, axis=-1, keepdims=True) * (1.0 / channels)
        inv_rms = lax.rsqrt(mean + 1e-06)
        place = lax.broadcasted_iota(jnp.int32, (CHUNK, 1), 0) + (base - reach * sec)
        low_end = (place >= 0) & (place < halo)
        high_end = (place >= span - halo) & (place < span)
        for m in range(1, micro):
            at = m * span
            low_end = low_end | ((place >= at) & (place < at + halo))
            high_end = high_end | ((place >= at + span - halo) & (place < at + span))
        outside = (low_end & (me == 0)) | (high_end & (me == peers - 1))
        inv_rms = jnp.where(outside, 0.0, inv_rms)

        for c in range(0, channels, col_tile):
            cols = slice(c, c + col_tile)
            normed = state_buf[LEAD : LEAD + CHUNK, cols] * inv_rms * gain_ref[:, cols]
            normed_buf[LEAD : LEAD + CHUNK, cols] = normed.astype(jnp.bfloat16).astype(jnp.float32)
            mixed = jnp.zeros((CHUNK, col_tile), jnp.float32)
            for k in range(taps):
                low = LEAD - 2 * reach + k
                mixed = mixed + taps_ref[k, :, cols] * normed_buf[low : low + CHUNK, cols]
            mixed_buf[:, cols] = mixed.astype(jnp.bfloat16)

        for c in range(0, channels, out_tile):
            cols = slice(c, c + out_tile)
            update = jnp.dot(
                mixed_buf[...], weight_ref[0, :, cols], preferred_element_type=jnp.float32
            )
            low = LEAD - reach
            result = state_buf[low : low + CHUNK, cols] + jax.nn.gelu(update)
            leaving[pl.ds(base, CHUNK), cols] = result.astype(jnp.bfloat16)

        @pl.when(jnp.logical_not(last))
        def _():
            state_copy(i).start()

        m = (i * CHUNK) // span

        @pl.when(((i + 1) * CHUNK) // span > m)
        def _():
            top = pl.multiple_of(m * span, 16)
            for c in range(0, channels, out_tile):
                cols = slice(c, c + out_tile)
                moved = jnp.dot(
                    order_ref[...],
                    leaving[pl.ds(top, span), cols],
                    preferred_element_type=jnp.float32,
                )
                ordered[m, :, :, cols] = moved.astype(jnp.bfloat16).reshape(
                    peers, share, out_tile
                )

            def send(k, carry):
                hint_copy(m, k).start()
                return carry

            lax.fori_loop(1, peers, send, 0)
            own_copy(m).start()

        return carry

    build_order()
    for load in loads:
        load.wait()
    lax.fori_loop(0, chunks, step, 0)

    @pl.when(jnp.logical_not(last))
    def _():
        def drain(i, carry):
            state_copy(i).wait_send()
            return carry

        lax.fori_loop(0, chunks, drain, 0)

    for m in range(micro):
        def finish(k, carry):
            copy = hint_copy(m, k)
            copy.wait_send()
            copy.wait_recv()
            return carry

        lax.fori_loop(1, peers, finish, 0)
        own_copy(m).wait()


def on_device(bases, stem_weight, norm_gain, conv_taps, proj_weight, dest):
    micro = bases.shape[0]
    rows = bases.shape[1] // BLOCK_BP
    channels = stem_weight.shape[1]
    sections = lax.axis_size("section")
    peers = lax.axis_size("seq")
    segs_dev = dest.shape[0]
    share = rows // peers
    taps = conv_taps.shape[1]
    reach = taps // 2
    halo = reach * sections
    span = rows + 2 * halo
    chunks = micro * span // CHUNK
    assert halo % 8 == 0 and (micro * span) % CHUNK == 0 and CHUNK <= span
    assert 2 * reach <= LEAD

    vmem = pl.BlockSpec(memory_space=pltpu.VMEM)
    hbm = pl.BlockSpec(memory_space=pl.ANY)
    dma = pltpu.SemaphoreType.DMA
    hints = pl.pallas_call(
        functools.partial(kernel, (micro, rows, halo, sections, peers, reach)),
        out_shape=jax.ShapeDtypeStruct((micro, peers, share, channels), jnp.bfloat16),
        in_specs=[vmem, hbm, hbm, hbm, hbm, vmem],
        out_specs=vmem,
        scratch_shapes=[
            pltpu.VMEM(stem_weight.shape, stem_weight.dtype),
            pltpu.VMEM(norm_gain.shape, norm_gain.dtype),
            pltpu.VMEM((taps, 1, channels), conv_taps.dtype),
            pltpu.VMEM(proj_weight.shape, proj_weight.dtype),
            pltpu.VMEM((rows, span), jnp.bfloat16),
            pltpu.VMEM((micro * span, BLOCK_BP), jnp.int32),
            pltpu.VMEM((micro * span, channels), jnp.bfloat16),
            pltpu.VMEM((micro * span, channels), jnp.bfloat16),
            pltpu.VMEM((micro, peers, share, channels), jnp.bfloat16),
            pltpu.VMEM((LEAD + CHUNK, channels), jnp.float32),
            pltpu.VMEM((LEAD + CHUNK, channels), jnp.float32),
            pltpu.VMEM((CHUNK, channels), jnp.bfloat16),
            dma((2, micro)),
            dma((2, micro)),
            dma((4,)),
            dma((chunks,)),
            dma((chunks,)),
            dma((micro, peers - 1)),
            dma((micro, peers - 1)),
            dma((micro,)),
        ],
        compiler_params=pltpu.CompilerParams(
            collective_id=0, has_side_effects=True, vmem_limit_bytes=60 * 1024 * 1024
        ),
    )(
        jnp.transpose(bases.reshape(micro, rows, BLOCK_BP), (1, 0, 2)),
        stem_weight,
        norm_gain,
        jnp.transpose(conv_taps, (1, 0, 2)),
        proj_weight,
        dest.reshape(1, segs_dev),
    )
    return hints.reshape(1, micro, rows, channels)


def solution(mesh):
    return jax.shard_map(
        on_device,
        mesh=mesh,
        in_specs=(
            P(None, "seq"),
            P(),
            P("section", None),
            P("section", None, None),
            P("section", None, None),
            P("seq"),
        ),
        out_specs=P("section", None, "seq", None),
        check_vma=False,
    )
```

```python
import functools

import jax
import jax.numpy as jnp
from jax import lax
from jax.experimental import pallas as pl
from jax.experimental.pallas import tpu as pltpu
from jax.sharding import PartitionSpec as P

BLOCK_BP = 128
CHUNK = 32
LEAD = 8
MESH = pl.DeviceIdType.MESH


def kernel(
    sizes,
    bases_ref,
    stem_hbm,
    gain_hbm,
    taps_hbm,
    weight_hbm,
    dest_ref,
    out_ref,
    stem_ref,
    gain_ref,
    taps_ref,
    weight_ref,
    order_ref,
    codes,
    arriving,
    leaving,
    ordered,
    state_buf,
    normed_buf,
    mixed_buf,
    codes_send,
    codes_recv,
    local_sem,
    state_send,
    state_recv,
    hint_send,
    hint_recv,
    own_sem,
):
    micro, rows, halo, sections, peers, reach = sizes
    channels = weight_ref.shape[1]
    segs_dev = dest_ref.shape[1]
    per_peer = segs_dev // peers
    seg_rows = rows // segs_dev
    span = rows + 2 * halo
    chunks = micro * span // CHUNK
    share = rows // peers
    taps = 2 * reach + 1
    sec = lax.axis_index("section")
    me = lax.axis_index("seq")
    first, last = sec == 0, sec == sections - 1
    col_tile = 256
    out_tile = 512

    loads = [
        pltpu.make_async_copy(src, dst, local_sem.at[n])
        for n, (src, dst) in enumerate(
            (
                (gain_hbm, gain_ref),
                (taps_hbm, taps_ref),
                (stem_hbm, stem_ref),
                (weight_hbm, weight_ref),
            )
        )
    ]
    for load in loads:
        load.start()

    barrier = pltpu.get_barrier_semaphore()

    def greet(k, carry):
        pl.semaphore_signal(
            barrier, inc=1, device_id={"seq": lax.rem(me + k, peers)}, device_id_type=MESH
        )
        return carry

    lax.fori_loop(1, peers, greet, 0)

    @pl.when(sec > 0)
    def _():
        pl.semaphore_signal(barrier, inc=1, device_id={"section": sec - 1}, device_id_type=MESH)

    @pl.when(first)
    def _():
        for m in range(micro):
            codes[m * span + halo : m * span + halo + rows] = bases_ref[:, m, :]

    state_buf[CHUNK : CHUNK + LEAD] = jnp.zeros((LEAD, channels), jnp.float32)
    normed_buf[CHUNK : CHUNK + LEAD] = jnp.zeros((LEAD, channels), jnp.float32)

    iota = functools.partial(lax.broadcasted_iota, jnp.int32)

    def zero_one(flags):
        return jnp.where(flags, 1.0, 0.0).astype(jnp.bfloat16)

    def build_order():
        dest_row = dest_ref[...]
        slot = lax.div(dest_row, segs_dev) * per_peer + lax.rem(
            lax.rem(dest_row, segs_dev), per_peer
        )
        runs = zero_one(iota((segs_dev, segs_dev), 0) == slot)
        by_slot = zero_one(
            lax.div(iota((rows, segs_dev), 0), seg_rows) == iota((rows, segs_dev), 1)
        )
        lag = halo + reach * (sec + 1)
        source = iota((segs_dev, span), 1) - lag
        by_run = zero_one(
            (source >= 0)
            & (lax.div(jnp.maximum(source, 0), seg_rows) == iota((segs_dev, span), 0))
        )
        picked = jnp.dot(by_slot, runs, preferred_element_type=jnp.float32).astype(jnp.bfloat16)
        picked = jnp.dot(picked, by_run, preferred_element_type=jnp.float32)
        phase = lax.rem(
            iota((rows, span), 0) - iota((rows, span), 1) + (lag + seg_rows * span), seg_rows
        )
        order_ref[...] = jnp.where(phase == 0, picked, 0.0).astype(jnp.bfloat16)

    build_order()

    @pl.when(last)
    def _():
        pl.semaphore_wait(barrier, peers - 1)

    @pl.when(jnp.logical_not(last))
    def _():
        pl.semaphore_wait(barrier, peers)

    def to_right(m):
        return pltpu.make_async_remote_copy(
            src_ref=codes.at[pl.ds(m * span + rows, halo)],
            dst_ref=codes.at[pl.ds(m * span, halo)],
            send_sem=codes_send.at[0, m],
            recv_sem=codes_recv.at[0, m],
            device_id={"seq": me + 1},
            device_id_type=MESH,
        )

    def to_left(m):
        return pltpu.make_async_remote_copy(
            src_ref=codes.at[pl.ds(m * span + halo, halo)],
            dst_ref=codes.at[pl.ds(m * span + halo + rows, halo)],
            send_sem=codes_send.at[1, m],
            recv_sem=codes_recv.at[1, m],
            device_id={"seq": me - 1},
            device_id_type=MESH,
        )

    @pl.when(first)
    def _():
        @pl.when(me < peers - 1)
        def _():
            for m in range(micro):
                to_right(m).start()

        @pl.when(me > 0)
        def _():
            for m in range(micro):
                to_left(m).start()

        @pl.when(me == 0)
        def _():
            for m in range(micro):
                codes[m * span : m * span + halo] = jnp.zeros((halo, BLOCK_BP), jnp.int32)

        @pl.when(me == peers - 1)
        def _():
            for m in range(micro):
                low = m * span + halo + rows
                codes[low : low + halo] = jnp.zeros((halo, BLOCK_BP), jnp.int32)

        @pl.when(me < peers - 1)
        def _():
            for m in range(micro):
                to_right(m).wait_send()
                to_left(m).wait_recv()

        @pl.when(me > 0)
        def _():
            for m in range(micro):
                to_left(m).wait_send()
                to_right(m).wait_recv()

    def state_copy(i):
        part = pl.ds(pl.multiple_of(i * CHUNK, CHUNK), CHUNK)
        return pltpu.make_async_remote_copy(
            src_ref=leaving.at[part],
            dst_ref=arriving.at[part],
            send_sem=state_send.at[i],
            recv_sem=state_recv.at[i],
            device_id={"section": sec + 1},
            device_id_type=MESH,
        )

    def hint_copy(m, k):
        peer = lax.rem(me + k, peers)
        return pltpu.make_async_remote_copy(
            src_ref=ordered.at[m, peer],
            dst_ref=out_ref.at[m, me],
            send_sem=hint_send.at[m, k - 1],
            recv_sem=hint_recv.at[m, k - 1],
            device_id={"seq": peer},
            device_id_type=MESH,
        )

    def own_copy(m):
        return pltpu.make_async_copy(ordered.at[m, me], out_ref.at[m, me], own_sem.at[m])

    def step(i, carry):
        base = pl.multiple_of(i * CHUNK, CHUNK)
        state_buf[0:LEAD] = state_buf[CHUNK : CHUNK + LEAD]
        normed_buf[0:LEAD] = normed_buf[CHUNK : CHUNK + LEAD]

        @pl.when(first)
        def _():
            code = codes[pl.ds(base, CHUNK)].astype(jnp.bfloat16)
            wide = 4 * BLOCK_BP
            spread = (
                lax.broadcasted_iota(jnp.int32, (BLOCK_BP, wide), 1) // 4
                == lax.broadcasted_iota(jnp.int32, (BLOCK_BP, wide), 0)
            )
            spread = jnp.where(spread, 1.0, 0.0).astype(jnp.bfloat16)
            repeated = jnp.dot(code, spread, preferred_element_type=jnp.float32)
            letter = lax.broadcasted_iota(jnp.int32, (CHUNK, wide), 1) % 4
            onehot = jnp.where(repeated == letter.astype(jnp.float32), 1.0, 0.0)
            onehot = onehot.astype(jnp.bfloat16)
            for c in range(0, channels, out_tile):
                part = jnp.dot(
                    onehot, stem_ref[:, c : c + out_tile], preferred_element_type=jnp.float32
                )
                state_buf[LEAD : LEAD + CHUNK, c : c + out_tile] = part.astype(
                    jnp.bfloat16
                ).astype(jnp.float32)

        @pl.when(jnp.logical_not(first))
        def _():
            state_copy(i).wait_recv()
            for c in range(0, channels, col_tile):
                state_buf[LEAD : LEAD + CHUNK, c : c + col_tile] = arriving[
                    pl.ds(base, CHUNK), c : c + col_tile
                ].astype(jnp.float32)

        total = jnp.zeros((CHUNK, 128), jnp.float32)
        for c in range(0, channels, 128):
            part = state_buf[LEAD : LEAD + CHUNK, c : c + 128]
            total = total + part * part
        mean = jnp.sum(total, axis=-1, keepdims=True) * (1.0 / channels)
        inv_rms = lax.rsqrt(mean + 1e-06)
        place = lax.broadcasted_iota(jnp.int32, (CHUNK, 1), 0) + (base - reach * sec)
        low_end = (place >= 0) & (place < halo)
        high_end = (place >= span - halo) & (place < span)
        for m in range(1, micro):
            at = m * span
            low_end = low_end | ((place >= at) & (place < at + halo))
            high_end = high_end | ((place >= at + span - halo) & (place < at + span))
        outside = (low_end & (me == 0)) | (high_end & (me == peers - 1))
        inv_rms = jnp.where(outside, 0.0, inv_rms)

        for c in range(0, channels, col_tile):
            cols = slice(c, c + col_tile)
            normed = state_buf[LEAD : LEAD + CHUNK, cols] * inv_rms * gain_ref[:, cols]
            normed_buf[LEAD : LEAD + CHUNK, cols] = normed.astype(jnp.bfloat16).astype(jnp.float32)
            mixed = jnp.zeros((CHUNK, col_tile), jnp.float32)
            for k in range(taps):
                low = LEAD - 2 * reach + k
                mixed = mixed + taps_ref[k, :, cols] * normed_buf[low : low + CHUNK, cols]
            mixed_buf[:, cols] = mixed.astype(jnp.bfloat16)

        for c in range(0, channels, out_tile):
            cols = slice(c, c + out_tile)
            update = jnp.dot(
                mixed_buf[...], weight_ref[0, :, cols], preferred_element_type=jnp.float32
            )
            low = LEAD - reach
            result = state_buf[low : low + CHUNK, cols] + jax.nn.gelu(update)
            leaving[pl.ds(base, CHUNK), cols] = result.astype(jnp.bfloat16)

        @pl.when(jnp.logical_not(last))
        def _():
            state_copy(i).start()

        m = (i * CHUNK) // span

        @pl.when(((i + 1) * CHUNK) // span > m)
        def _():
            top = pl.multiple_of(m * span, 16)
            for c in range(0, channels, out_tile):
                cols = slice(c, c + out_tile)
                moved = jnp.dot(
                    order_ref[...],
                    leaving[pl.ds(top, span), cols],
                    preferred_element_type=jnp.float32,
                )
                ordered[m, :, :, cols] = moved.astype(jnp.bfloat16).reshape(
                    peers, share, out_tile
                )

            def send(k, carry):
                hint_copy(m, k).start()
                return carry

            lax.fori_loop(1, peers, send, 0)
            own_copy(m).start()

        return carry

    for load in loads:
        load.wait()
    lax.fori_loop(0, chunks, step, 0)

    @pl.when(jnp.logical_not(last))
    def _():
        def drain(i, carry):
            state_copy(i).wait_send()
            return carry

        lax.fori_loop(0, chunks, drain, 0)

    for m in range(micro):
        def finish(k, carry):
            copy = hint_copy(m, k)
            copy.wait_send()
            copy.wait_recv()
            return carry

        lax.fori_loop(1, peers, finish, 0)
        own_copy(m).wait()


def on_device(bases, stem_weight, norm_gain, conv_taps, proj_weight, dest):
    micro = bases.shape[0]
    rows = bases.shape[1] // BLOCK_BP
    channels = stem_weight.shape[1]
    sections = lax.axis_size("section")
    peers = lax.axis_size("seq")
    segs_dev = dest.shape[0]
    share = rows // peers
    taps = conv_taps.shape[1]
    reach = taps // 2
    halo = reach * sections
    span = rows + 2 * halo
    chunks = micro * span // CHUNK
    assert halo % 8 == 0 and (micro * span) % CHUNK == 0 and CHUNK <= span
    assert 2 * reach <= LEAD

    vmem = pl.BlockSpec(memory_space=pltpu.VMEM)
    hbm = pl.BlockSpec(memory_space=pl.ANY)
    dma = pltpu.SemaphoreType.DMA
    hints = pl.pallas_call(
        functools.partial(kernel, (micro, rows, halo, sections, peers, reach)),
        out_shape=jax.ShapeDtypeStruct((micro, peers, share, channels), jnp.bfloat16),
        in_specs=[vmem, hbm, hbm, hbm, hbm, vmem],
        out_specs=vmem,
        scratch_shapes=[
            pltpu.VMEM(stem_weight.shape, stem_weight.dtype),
            pltpu.VMEM(norm_gain.shape, norm_gain.dtype),
            pltpu.VMEM((taps, 1, channels), conv_taps.dtype),
            pltpu.VMEM(proj_weight.shape, proj_weight.dtype),
            pltpu.VMEM((rows, span), jnp.bfloat16),
            pltpu.VMEM((micro * span, BLOCK_BP), jnp.int32),
            pltpu.VMEM((micro * span, channels), jnp.bfloat16),
            pltpu.VMEM((micro * span, channels), jnp.bfloat16),
            pltpu.VMEM((micro, peers, share, channels), jnp.bfloat16),
            pltpu.VMEM((LEAD + CHUNK, channels), jnp.float32),
            pltpu.VMEM((LEAD + CHUNK, channels), jnp.float32),
            pltpu.VMEM((CHUNK, channels), jnp.bfloat16),
            dma((2, micro)),
            dma((2, micro)),
            dma((4,)),
            dma((chunks,)),
            dma((chunks,)),
            dma((micro, peers - 1)),
            dma((micro, peers - 1)),
            dma((micro,)),
        ],
        compiler_params=pltpu.CompilerParams(
            collective_id=0, has_side_effects=True, vmem_limit_bytes=60 * 1024 * 1024
        ),
    )(
        jnp.transpose(bases.reshape(micro, rows, BLOCK_BP), (1, 0, 2)),
        stem_weight,
        norm_gain,
        jnp.transpose(conv_taps, (1, 0, 2)),
        proj_weight,
        dest.reshape(1, segs_dev),
    )
    return hints.reshape(1, micro, rows, channels)


def solution(mesh):
    return jax.shard_map(
        on_device,
        mesh=mesh,
        in_specs=(
            P(None, "seq"),
            P(),
            P("section", None),
            P("section", None, None),
            P("section", None, None),
            P("seq"),
        ),
        out_specs=P("section", None, "seq", None),
        check_vma=False,
    )
```
